32 devices in a mesh: ctx: 16 (over z, x, core), head: 2 (over y).
Axes of the slice: x: 2, y: 2, z: 4, core: 2. Of those that a mesh axis runs over, the one named last changes fastest.
Arguments:
- tokens: bfloat16 [4096, 768], P('ctx'), may hold values from -6 to 6
- w_qkv: bfloat16 [768, 3, 768], P('ctx', None, 'head'), may hold values from -0.3125 to 0.3125
- w_out: bfloat16 [768, 768], P('head', 'ctx'), may hold values from -1.25 to 1.25
- w_in: bfloat16 [768, 2, 1152], P('ctx', None, 'head'), may hold values from -0.21875 to 0.21875
- w_down: bfloat16 [1152, 768], P('head', 'ctx'), may hold values from -0.1875 to 0.1875
- gain_attn: bfloat16 [768], P('ctx'), may hold values from 0.099609375 to 1.8984375
- gain_mlp: bfloat16 [768], P('ctx'), may hold values from 0.099609375 to 1.8984375
- cotangent: bfloat16 [4096, 768], P('ctx'), may hold values from -6 to 6
Outputs:
- mixed: bfloat16 [4096, 768], P('ctx')
- grad_tokens: float32 [4096, 768], P('ctx')
- grad_qkv: float32 [768, 3, 768], P('ctx', None, 'head')
- grad_out: float32 [768, 768], P('head', 'ctx')
- grad_in: float32 [768, 2, 1152], P('ctx', None, 'head')
- grad_down: float32 [1152, 768], P('head', 'ctx')
- grad_gain_attn: float32 [768], P('ctx')
- grad_gain_mlp: float32 [768], P('ctx')
The draws below stay inside these ranges and needn't reach their ends.
All inputs are finite; a program needn't handle non-finite values.
Results may differ from the reference program's by a relative error of at most 0.019.
The reference program's roundings to bfloat16 on the way count: a program that leaves them out, or rounds other values in their place, can miss the bound.
Values may be sent and summed in bfloat16 or wider, within the bound.
A program may use at most 192 MiB of HBM per device.

```python
import jax
import jax.numpy as jnp
from jax import lax

D = 768
HEADS = 12
HEAD_DIM = 64
FF = 1152
TOKENS = 4096


def steps_of(own_key, dims, cuts, smallest, largest):
    def one(axis_at, shards_of):
        steps = jax.random.uniform(jax.random.fold_in(jax.random.fold_in(own_key, 6), axis_at), (shards_of,), jnp.float32, smallest / len(cuts), largest / len(cuts))
        return jnp.repeat(jnp.exp(steps), dims[axis_at] // shards_of).reshape((-1,) + (1,) * (len(dims) - axis_at - 1))

    level = one(*cuts[0])
    for cut in cuts[1:]:
        level = level * one(*cut)
    return level


def bell_draw(own_key, shape, width, most, cuts=(), kind=jnp.bfloat16):
    factor_of = steps_of(own_key, shape, cuts, -0.22, 0.18) if cuts else 1.0
    array = jax.random.normal(own_key, shape, jnp.float32) * width * factor_of
    return jnp.minimum(jnp.maximum(array, -most), most).astype(kind)


def setup_inputs(seed: int = 0) -> dict:
    key_list = jax.random.split(jax.random.key(seed), 9)
    tokens = bell_draw(key_list[0], (TOKENS, D), 1.0, 6.0, ((0, 16),))
    w_qkv = bell_draw(key_list[1], (D, 3, D), (D // 2) ** -0.5, 0.3125, ((0, 16), (2, 2)))
    w_out = bell_draw(key_list[2], (D, D), (max(1, 110 * D // TOKENS)) ** -0.5, 1.25, ((0, 2), (1, 16)))
    w_in = bell_draw(key_list[3], (D, 2, FF), D ** -0.5, 0.21875, ((0, 16), (2, 2)))
    w_down = bell_draw(key_list[4], (FF, D), FF ** -0.5, 0.1875, ((0, 2), (1, 16)))
    gain_attn = jnp.clip(1.0 + 0.18 * jax.random.normal(key_list[5], (D,), jnp.float32), 0.099609375, 1.8984375).astype(jnp.bfloat16)
    gain_mlp = jnp.clip(1.0 + 0.18 * jax.random.normal(key_list[6], (D,), jnp.float32), 0.099609375, 1.8984375).astype(jnp.bfloat16)
    cotangent = bell_draw(key_list[7], (TOKENS, D), 1.0, 6.0, ((0, 16),))
    return {"tokens": tokens, "w_qkv": w_qkv, "w_out": w_out, "w_in": w_in, "w_down": w_down, "gain_attn": gain_attn, "gain_mlp": gain_mlp, "cotangent": cotangent}


@jax.custom_vjp
def low(v):
    return lax.optimization_barrier(v.astype(jnp.bfloat16)).astype(jnp.float32)

@jax.custom_vjp
def low_back(v):
    return v

def low_keep(v):
    return (low(v), None)

def low_pass(kept, grad):
    return (grad,)

def back_keep(v):
    return (v, None)

def back_low(kept, grad):
    return (low(grad),)
low.defvjp(low_keep, low_pass)
low_back.defvjp(back_keep, back_low)
rope_base = 160000.0
epsilon = 1e-05
highest = lax.Precision.HIGHEST

def layer_norm(values, gain):
    centred = values - lax.optimization_barrier(jnp.mean(values, axis=-1, keepdims=True))
    spread = lax.optimization_barrier(jnp.mean(centred * centred, axis=-1, keepdims=True))
    return centred * lax.rsqrt(spread + epsilon) * gain

def rope_tables():
    positions = jnp.arange(TOKENS, dtype=jnp.int32).astype(jnp.float32)
    exponent = jnp.arange(HEAD_DIM // 2, dtype=jnp.int32).astype(jnp.float32) * (2.0 / HEAD_DIM)
    inverse = rope_base ** (-exponent)
    angles = positions[:, None] * inverse[None, :]
    angles = jnp.concatenate([angles, angles], axis=1)[:, None, :]
    return (jnp.cos(angles), jnp.sin(angles))

def rotate(values, cosine, sine):
    half = values.shape[-1] // 2
    turned = jnp.concatenate([-values[..., half:], values[..., :half]], axis=-1)
    return values * cosine + turned * sine

def attention(queries, keys, values):
    block_count = max(1, TOKENS // 512)
    block_rows = TOKENS // block_count
    scale = HEAD_DIM ** (-0.5)
    blocks = queries.reshape(block_count, block_rows, HEADS, HEAD_DIM)

    def one_block(block):
        scores = jnp.einsum('bhe,the->hbt', block, keys, precision=highest) * scale
        scores = low_back(scores)
        probs = low(jax.nn.softmax(scores, axis=-1))
        return jnp.einsum('hbt,the->bhe', probs, values, precision=highest)
    outcome = lax.map(jax.checkpoint(one_block), blocks)
    return outcome.reshape(TOKENS, D)

def forward(tokens, w_qkv, w_out, w_in, w_down, gain_attn, gain_mlp):
    normed = low(layer_norm(tokens, gain_attn))
    mixed_qkv = low_back(jnp.einsum('td,dcf->tcf', normed, w_qkv, precision=highest))
    cosine, sine = rope_tables()
    queries = low(rotate(mixed_qkv[:, 0].reshape(TOKENS, HEADS, HEAD_DIM), cosine, sine))
    keys = low(rotate(mixed_qkv[:, 1].reshape(TOKENS, HEADS, HEAD_DIM), cosine, sine))
    values = low(mixed_qkv[:, 2].reshape(TOKENS, HEADS, HEAD_DIM))
    attended = low(low_back(attention(queries, keys, values)))
    branch = low_back(jnp.dot(attended, w_out, precision=highest))
    middle = tokens + branch
    normed_mlp = low(layer_norm(middle, gain_mlp))
    gate_up = low_back(jnp.einsum('td,dcf->tcf', normed_mlp, w_in, precision=highest))
    hidden = low(jax.nn.gelu(gate_up[:, 0], approximate=False) * gate_up[:, 1])
    return middle + low_back(jnp.dot(hidden, w_down, precision=highest))

def reference(tokens, w_qkv, w_out, w_in, w_down, gain_attn, gain_mlp, cotangent):
    inputs = (tokens.astype(jnp.float32), w_qkv.astype(jnp.float32), w_out.astype(jnp.float32), w_in.astype(jnp.float32), w_down.astype(jnp.float32), gain_attn.astype(jnp.float32), gain_mlp.astype(jnp.float32))
    result, pull = jax.vjp(forward, *inputs)
    grads = pull(cotangent.astype(jnp.float32))
    return (result.astype(jnp.bfloat16), grads[0], grads[1], grads[2], grads[3], grads[4], grads[5], grads[6])
```

```python
import functools

import jax
import jax.numpy as jnp
from jax import lax
from jax.experimental import pallas as pl
from jax.experimental.pallas import tpu as pltpu
from jax.sharding import PartitionSpec as P

HEAD_DIM = 64
PAIR = 2 * HEAD_DIM
MESH = pl.DeviceIdType.MESH
VMEM_LIMIT = 56 * 1024 * 1024
RESIDENT_LIMIT = 32 * 1024 * 1024

rope_base = 160000.0
epsilon = 1e-05
f32 = jnp.float32
bf16 = jnp.bfloat16


def layer_norm(values, gain):
    centred = values - jnp.mean(values, axis=-1, keepdims=True)
    spread = jnp.mean(centred * centred, axis=-1, keepdims=True)
    return centred * lax.rsqrt(spread + epsilon) * gain


def rope_tables(first, rows):
    positions = (first + jnp.arange(rows, dtype=jnp.int32)).astype(f32)
    exponent = jnp.arange(HEAD_DIM // 2, dtype=jnp.int32).astype(f32) * (2.0 / HEAD_DIM)
    inverse = rope_base ** (-exponent)
    angles = positions[:, None] * inverse[None, :]
    angles = jnp.concatenate([angles, angles], axis=1)[:, None, :]
    return (jnp.cos(angles), jnp.sin(angles))


def turn_half(values):
    half = values.shape[-1] // 2
    return jnp.concatenate([-values[..., half:], values[..., :half]], axis=-1)


def rotate(values, cosine, sine):
    return values * cosine + turn_half(values) * sine


def unrotate(values, cosine, sine):
    return values * cosine - turn_half(values) * sine


def split_heads(flat_rows):
    return flat_rows.reshape(flat_rows.shape[0], -1, HEAD_DIM)


class Ring:
    def __init__(self, devices):
        self.chips = devices // 2
        self.rights = self.chips // 2
        self.lefts = self.chips - 1 - self.rights
        self.me = lax.axis_index("ctx")
        self.head = lax.axis_index("head")
        chip = lax.div(self.me, 2)
        self.core = lax.rem(self.me, 2)
        side = lax.rem(chip, 2)
        level = lax.div(chip, 2)
        self.place = level + side * (self.chips - 1 - 2 * level)

    def chip_at(self, place):
        place = lax.rem(place + 2 * self.chips, self.chips)
        far = lax.div(place, self.chips // 2)
        return (1 - far) * 2 * place + far * (2 * (self.chips - 1 - place) + 1)

    def index(self, offset, core):
        return self.chip_at(self.place + offset) * 2 + core

    def neighbours(self):
        return (self.index(1, self.core), self.index(-1, self.core), self.me + 1 - 2 * self.core)

    def barrier(self):
        sem = pltpu.get_barrier_semaphore()
        for other in self.neighbours():
            pl.semaphore_signal(sem, inc=1, device_id=(other, self.head), device_id_type=MESH)
        pl.semaphore_wait(sem, 3)


class Gather:
    def __init__(self, ring, own, full, send, recv, local):
        self.ring, self.own, self.full = ring, own, full
        self.send, self.recv, self.local = send, recv, local
        self.right, self.left, self.sibling = ring.neighbours()

    def copies(self, kind, number, slot, target, first=False):
        return [
            pltpu.make_async_remote_copy(
                src_ref=own if first else full.at[slot],
                dst_ref=full.at[slot],
                send_sem=self.send.at[a, kind, number],
                recv_sem=self.recv.at[a, kind, number],
                device_id=(target, self.ring.head),
                device_id_type=MESH,
            )
            for a, (own, full) in enumerate(zip(self.own, self.full))
        ]

    def start(self, *where, first=False):
        for copy in self.copies(*where, first=first):
            copy.start()

    def arrive(self, kind, number, slot):
        for copy in self.copies(kind, number, slot, self.sibling):
            copy.wait_recv()

    def begin(self):
        ring = self.ring
        self.start(0, 0, ring.me, self.right, first=True)
        self.start(1, 0, ring.me, self.left, first=True)
        self.start(2, 0, ring.me, self.sibling, first=True)
        for a, (own, full) in enumerate(zip(self.own, self.full)):
            copy = pltpu.make_async_copy(own, full.at[ring.me], self.local.at[a])
            copy.start()
            copy.wait()

    def step(self, s):
        ring = self.ring
        slot = ring.index(-s, ring.core)
        self.arrive(0, s - 1, slot)

        @pl.when(s < ring.rights)
        def _():
            self.start(0, s, slot, self.right)

        self.start(2, s, slot, self.sibling)

        @pl.when(s <= ring.lefts)
        def _():
            other = ring.index(s, ring.core)
            self.arrive(1, s - 1, other)

            @pl.when(s < ring.lefts)
            def _():
                self.start(1, s, other, self.left)

            self.start(2, ring.rights + s, other, self.sibling)

    def sibling_step(self, s):
        ring = self.ring
        self.arrive(2, s, ring.index(-s, 1 - ring.core))

        @pl.when(s <= ring.lefts)
        def _():
            self.arrive(2, ring.rights + s, ring.index(s, 1 - ring.core))

    def sibling_first(self):
        self.arrive(2, 0, self.sibling)

    def finish(self):
        ring = self.ring

        def sent(kind):
            def one(number, carry):
                for copy in self.copies(kind, number, ring.me, self.sibling):
                    copy.wait_send()
                return carry

            return one

        lax.fori_loop(0, ring.rights, sent(0), 0)
        lax.fori_loop(0, ring.lefts, sent(1), 0)
        lax.fori_loop(0, ring.chips, sent(2), 0)


def gather_sems(arrays, devices):
    chips = devices // 2
    return [
        pltpu.SemaphoreType.DMA((arrays, 3, chips)),
        pltpu.SemaphoreType.DMA((arrays, 3, chips)),
        pltpu.SemaphoreType.DMA((arrays,)),
    ]


def params(number):
    return pltpu.CompilerParams(
        collective_id=number, has_side_effects=True, vmem_limit_bytes=VMEM_LIMIT
    )


whole_vmem = pl.BlockSpec(memory_space=pltpu.VMEM)
whole_any = pl.BlockSpec(memory_space=pl.ANY)


def gather_kernel(devices, own, full, send, recv, local):
    ring = Ring(devices)
    ring.barrier()
    gather = Gather(ring, [own], [full], send, recv, local)
    gather.begin()
    gather.sibling_first()

    def step(s, carry):
        gather.step(s)
        return carry

    lax.fori_loop(1, ring.rights + 1, step, 0)

    def late(s, carry):
        gather.sibling_step(s)
        return carry

    lax.fori_loop(1, ring.rights + 1, late, 0)
    gather.finish()


def all_gather(own, devices, number):
    return pl.pallas_call(
        functools.partial(gather_kernel, devices),
        out_shape=jax.ShapeDtypeStruct((devices,) + own.shape, own.dtype),
        in_specs=[whole_any],
        out_specs=whole_any,
        scratch_shapes=gather_sems(1, devices),
        compiler_params=params(number),
    )(own)


def nt(a, b):
    return lax.dot_general(a, b, (((1,), (1,)), ((), ())), preferred_element_type=f32)


def nn(a, b):
    return jnp.dot(a, b, preferred_element_type=f32)


def lane_mask(rows, side):
    lanes = lax.broadcasted_iota(jnp.int32, (rows, PAIR), 1)
    return (lanes >= HEAD_DIM) if side else (lanes < HEAD_DIM)


def masked_heads(source, offset, heads, target):
    for h in range(heads):
        start = offset + (h // 2) * PAIR
        block = source[:, start : start + PAIR].astype(f32)
        keep = lane_mask(block.shape[0], h % 2)
        target[h] = jnp.where(keep, block, 0.0).astype(bf16)


def visit(ring, gather, process):
    gather.begin()
    process(ring.me)
    gather.sibling_first()
    process(gather.sibling)

    def step(s, carry):
        gather.step(s)

        def half(other, carry):
            @pl.when(other == 1)
            def _():
                gather.sibling_step(s)

            core = ring.core + other * (1 - 2 * ring.core)
            ways = jnp.where(s <= ring.lefts, 2, 1)

            def way(w, carry):
                process(ring.index((2 * w - 1) * s, core))
                return carry

            return lax.fori_loop(0, ways, way, carry)

        return lax.fori_loop(0, 2, half, carry)

    lax.fori_loop(1, ring.rights + 1, step, 0)
    gather.finish()


def forward_kernel(devices, heads, q, kv, full, att, lse, qm, top, total, acc, send, recv, local, *stage):
    width = heads * HEAD_DIM
    ring = Ring(devices)
    ring.barrier()
    gather = Gather(ring, [kv], [full], send, recv, local)
    masked_heads(q, 0, heads, qm)
    top[...] = jnp.full_like(top, -1e30)
    total[...] = jnp.zeros_like(total)
    acc[...] = jnp.zeros_like(acc)

    def process(slot):
        block = full.at[slot]
        if stage:
            copy = pltpu.make_async_copy(block, stage[0], stage[1])
            copy.start()
            copy.wait()
            block = stage[0]
        for p in range(heads // 2):
            keys = block[:, p * PAIR : (p + 1) * PAIR]
            values = block[:, width + p * PAIR : width + (p + 1) * PAIR].T
            for side in range(2):
                h = 2 * p + side
                scores = nt(keys, qm[h])
                before = top[h : h + 1]
                peak = jnp.maximum(before, jnp.max(scores, axis=0, keepdims=True))
                shrink = jnp.exp(before - peak)
                weights = jnp.exp(scores - peak)
                top[h : h + 1] = peak
                total[h : h + 1] = total[h : h + 1] * shrink + jnp.sum(
                    weights, axis=0, keepdims=True
                )
                part = nn(values[side * HEAD_DIM : (side + 1) * HEAD_DIM], weights.astype(bf16))
                rows = slice(h * HEAD_DIM, (h + 1) * HEAD_DIM)
                acc[rows] = acc[rows] * shrink + part

    visit(ring, gather, process)
    for h in range(heads):
        rows = slice(h * HEAD_DIM, (h + 1) * HEAD_DIM)
        acc[rows] = acc[rows] / total[h : h + 1]
    att[...] = acc[...].T
    lse[...] = top[...] + jnp.log(jnp.maximum(total[...], 1e-37))


def resident(devices, rows, width):
    return devices * rows * width * 2 * 2 <= RESIDENT_LIMIT


def forward_attention(q, kv, devices, number):
    rows, width = q.shape
    heads = width // HEAD_DIM
    near = resident(devices, rows, 2 * width)
    return pl.pallas_call(
        functools.partial(forward_kernel, devices, heads),
        out_shape=(
            jax.ShapeDtypeStruct((devices,) + kv.shape, bf16),
            jax.ShapeDtypeStruct((rows, width), f32),
            jax.ShapeDtypeStruct((8, rows), f32),
        ),
        in_specs=[whole_vmem, whole_vmem if near else whole_any],
        out_specs=(whole_vmem if near else whole_any, whole_vmem, whole_vmem),
        scratch_shapes=[
            pltpu.VMEM((heads, rows, PAIR), bf16),
            pltpu.VMEM((8, rows), f32),
            pltpu.VMEM((8, rows), f32),
            pltpu.VMEM((width, rows), f32),
        ]
        + gather_sems(1, devices)
        + ([] if near else [pltpu.VMEM(kv.shape, bf16), pltpu.SemaphoreType.DMA]),
        compiler_params=params(number),
    )(q, kv)


def backward_kernel(
    devices, heads, qg, stats, kv, kv_all, dq, dk, dv, *rest
):
    full, stats_all = rest[:2]
    rest = rest[2:]
    qm, gm, km, vm, dqt, dka, dva, send, recv, local = rest[:10]
    stage = rest[10:]
    width = heads * HEAD_DIM
    ring = Ring(devices)
    ring.barrier()
    gather = Gather(ring, [qg, stats], [full, stats_all], send, recv, local)
    own = qg
    if stage:
        copies = [
            pltpu.make_async_copy(qg, stage[0], stage[3].at[0]),
            pltpu.make_async_copy(stats, stage[4], stage[3].at[1]),
        ]
        for copy in copies:
            copy.start()
        for copy in copies:
            copy.wait()
        own = stage[0]
    mine = stage[4] if stage else stats
    masked_heads(own, 0, heads, qm)
    masked_heads(own, width, heads, gm)
    masked_heads(kv, 0, heads, km)
    masked_heads(kv, width, heads, vm)
    dqt[...] = jnp.zeros_like(dqt)
    dka[...] = jnp.zeros_like(dka)
    dva[...] = jnp.zeros_like(dva)

    def process(slot):
        block, keyed, rows_of = full.at[slot], kv_all.at[slot], stats_all.at[slot]
        if stage:
            copies = [
                pltpu.make_async_copy(block, stage[0], stage[3].at[0]),
                pltpu.make_async_copy(keyed, stage[1], stage[3].at[1]),
                pltpu.make_async_copy(rows_of, stage[2], stage[3].at[2]),
            ]
            for copy in copies:
                copy.start()
            for copy in copies:
                copy.wait()
            block, keyed, rows_of = stage[:3]
        for p in range(heads // 2):
            first = slice(p * PAIR, (p + 1) * PAIR)
            second = slice(width + p * PAIR, width + (p + 1) * PAIR)
            keys = keyed[:, first]
            values = keyed[:, second]
            turned = keys.T
            queries = block[:, first]
            grads = block[:, second]
            for side in range(2):
                h = 2 * p + side
                probs = jnp.exp(nt(keys, qm[h]) - mine[h : h + 1])
                slope = nt(values, gm[h])
                small = (probs * (slope - mine[8 + h : 9 + h])).astype(bf16)
                rows = slice(h * HEAD_DIM, (h + 1) * HEAD_DIM)
                dqt[rows] += nn(turned[side * HEAD_DIM : (side + 1) * HEAD_DIM], small)
                probs = jnp.exp(nt(km[h], queries) - rows_of[h : h + 1])
                slope = nt(vm[h], grads)
                small = (probs * (slope - rows_of[8 + h : 9 + h])).astype(bf16)
                dva[h] += nn(probs.astype(bf16), grads)
                dka[h] += nn(small, queries)

    visit(ring, gather, process)
    dq[...] = dqt[...].T * (HEAD_DIM ** (-0.5))
    keep = lane_mask(dk.shape[0], 0)
    for p in range(heads // 2):
        first = slice(p * PAIR, (p + 1) * PAIR)
        dk[:, first] = jnp.where(keep, dka[2 * p], dka[2 * p + 1])
        dv[:, first] = jnp.where(keep, dva[2 * p], dva[2 * p + 1])


def backward_attention(qg, stats, kv, kv_all, devices, number):
    rows = qg.shape[0]
    width = qg.shape[1] // 2
    heads = width // HEAD_DIM
    near = resident(devices, rows, 2 * width)
    flat = jax.ShapeDtypeStruct((rows, width), f32)
    out_shape = [flat, flat, flat]
    out_specs = [whole_vmem] * 3
    buffers = []
    if near:
        buffers = [
            pltpu.VMEM((devices,) + qg.shape, bf16),
            pltpu.VMEM((devices,) + stats.shape, f32),
        ]
    else:
        out_shape += [
            jax.ShapeDtypeStruct((devices,) + qg.shape, bf16),
            jax.ShapeDtypeStruct((devices,) + stats.shape, f32),
        ]
        out_specs += [whole_any] * 2
    space = whole_vmem if near else whole_any
    return pl.pallas_call(
        functools.partial(backward_kernel, devices, heads),
        out_shape=tuple(out_shape),
        in_specs=[space, space, whole_vmem, space],
        out_specs=tuple(out_specs),
        scratch_shapes=buffers
        + [
            pltpu.VMEM((heads, rows, PAIR), bf16),
            pltpu.VMEM((heads, rows, PAIR), bf16),
            pltpu.VMEM((heads, rows, PAIR), bf16),
            pltpu.VMEM((heads, rows, PAIR), bf16),
            pltpu.VMEM((width, rows), f32),
            pltpu.VMEM((heads, rows, PAIR), f32),
            pltpu.VMEM((heads, rows, PAIR), f32),
        ]
        + gather_sems(2, devices)
        + (
            []
            if near
            else [
                pltpu.VMEM(qg.shape, bf16),
                pltpu.VMEM(kv.shape, bf16),
                pltpu.VMEM(stats.shape, f32),
                pltpu.SemaphoreType.DMA((3,)),
                pltpu.VMEM(stats.shape, f32),
            ]
        ),
        compiler_params=params(number),
    )(qg, stats, kv, kv_all)[:3]


def exchange_kernel(own, out, arrived, send, recv):
    other = 1 - lax.axis_index("head")
    here = lax.axis_index("ctx")
    sem = pltpu.get_barrier_semaphore()
    pl.semaphore_signal(sem, inc=1, device_id=(here, other), device_id_type=MESH)
    pl.semaphore_wait(sem, 1)
    copy = pltpu.make_async_remote_copy(
        src_ref=own, dst_ref=arrived, send_sem=send, recv_sem=recv,
        device_id=(here, other), device_id_type=MESH,
    )
    copy.start()
    copy.wait()
    out[...] = own[...].astype(f32) + arrived[...].astype(f32)


def head_sum(part, number):
    part = part.astype(bf16)
    return pl.pallas_call(
        exchange_kernel,
        out_shape=jax.ShapeDtypeStruct(part.shape, f32),
        in_specs=[whole_vmem],
        out_specs=whole_vmem,
        scratch_shapes=[
            pltpu.VMEM(part.shape, bf16), pltpu.SemaphoreType.DMA, pltpu.SemaphoreType.DMA,
        ],
        compiler_params=params(number),
    )(part)


def scatter_kernel(devices, part, out, stage, rights, lefts, send, recv):
    ring = Ring(devices)
    right, left, sibling = ring.neighbours()
    ring.barrier()

    def make(source, target, kind, number, device):
        return pltpu.make_async_remote_copy(
            src_ref=source, dst_ref=target,
            send_sem=send.at[kind, number], recv_sem=recv.at[kind, number],
            device_id=(device, ring.head), device_id_type=MESH,
        )

    def launch_chip(step, carry):
        chip = ring.chip_at(ring.place + ring.rights - step)
        make(part.at[chip * 2 + 1 - ring.core], stage.at[chip], 2, chip, sibling).start()
        return carry

    lax.fori_loop(0, ring.chips, launch_chip, 0)

    def landed(step, carry):
        chip = ring.chip_at(ring.place + ring.rights - step)
        make(part.at[chip * 2 + 1 - ring.core], stage.at[chip], 2, chip, sibling).wait()
        stage[chip] = (
            stage[chip].astype(f32) + part[chip * 2 + ring.core].astype(f32)
        ).astype(bf16)
        return carry

    lax.fori_loop(0, ring.chips, landed, 0)
    make(stage.at[ring.chip_at(ring.place + ring.rights)], rights.at[0], 0, 0, right).start()
    make(stage.at[ring.chip_at(ring.place - ring.lefts)], lefts.at[0], 1, 0, left).start()

    def step(s, carry):
        make(rights.at[s - 1], rights.at[s - 1], 0, s - 1, right).wait_recv()
        chip = ring.chip_at(ring.place + ring.rights - s)
        rights[s - 1] = (rights[s - 1].astype(f32) + stage[chip].astype(f32)).astype(bf16)
        make(rights.at[s - 1], rights.at[s], 0, s, right).start()

        @pl.when(s < ring.lefts)
        def _():
            make(lefts.at[s - 1], lefts.at[s - 1], 1, s - 1, left).wait_recv()
            chip = ring.chip_at(ring.place - ring.lefts + s)
            lefts[s - 1] = (lefts[s - 1].astype(f32) + stage[chip].astype(f32)).astype(bf16)
            make(lefts.at[s - 1], lefts.at[s], 1, s, left).start()

        return carry

    lax.fori_loop(1, ring.rights, step, 0)
    make(lefts.at[ring.lefts - 1], lefts.at[ring.lefts - 1], 1, ring.lefts - 1, left).wait_recv()
    make(rights.at[ring.rights - 1], rights.at[ring.rights - 1], 0, ring.rights - 1, right).wait_recv()
    out[...] = (
        stage[ring.chip_at(ring.place)].astype(f32)
        + rights[ring.rights - 1].astype(f32)
        + lefts[ring.lefts - 1].astype(f32)
    )

    def sent(kind):
        def one(number, carry):
            make(stage.at[0], stage.at[0], kind, number, right).wait_send()
            return carry

        return one

    lax.fori_loop(0, ring.rights, sent(0), 0)
    lax.fori_loop(0, ring.lefts, sent(1), 0)


def reduce_scatter(part, devices, number):
    block = part.shape[1:]
    chips = devices // 2
    return pl.pallas_call(
        functools.partial(scatter_kernel, devices),
        out_shape=jax.ShapeDtypeStruct(block, f32),
        in_specs=[whole_vmem],
        out_specs=whole_vmem,
        scratch_shapes=[
            pltpu.VMEM((chips,) + block, bf16),
            pltpu.VMEM((chips // 2,) + block, bf16),
            pltpu.VMEM((chips // 2,) + block, bf16),
            pltpu.SemaphoreType.DMA((3, chips)),
            pltpu.SemaphoreType.DMA((3, chips)),
        ],
        compiler_params=params(number),
    )(part)


def shards(devices, tokens, w_qkv, w_out, w_in, w_down, gain_attn, gain_mlp, cotangent):
    rows, wide = tokens.shape
    own = w_qkv.shape[0]
    scale = HEAD_DIM ** (-0.5)
    width_here = w_qkv.shape[2]
    hidden_here = w_in.shape[2]
    sizes = (3 * width_here, 2 * hidden_here, width_here, hidden_here, 1, 1)
    marks = [sum(sizes[:i]) for i in range(len(sizes) + 1)]
    spare = -marks[-1] % 128
    packed = jnp.concatenate(
        [
            w_qkv.reshape(own, -1),
            w_in.reshape(own, -1),
            w_out.T,
            w_down.T,
            gain_attn[:, None],
            gain_mlp[:, None],
            jnp.zeros((own, spare), bf16),
        ],
        axis=1,
    )
    everything = all_gather(packed, devices, 0).reshape(wide, -1)
    full_qkv, full_in, out_turned, down_turned = (
        everything[:, marks[i] : marks[i + 1]] for i in range(4)
    )
    gain_first = everything[:, marks[4]].astype(f32)
    gain_second = everything[:, marks[5]].astype(f32)
    cosine, sine = rope_tables(lax.axis_index("ctx") * rows, rows)
    inputs = tokens.astype(f32)
    normed = layer_norm(inputs, gain_first).astype(bf16)
    mixed_qkv = nn(normed, full_qkv).reshape(rows, 3, width_here)
    query_heads = rotate(split_heads(mixed_qkv[:, 0]), cosine, sine).astype(bf16)
    key_heads = rotate(split_heads(mixed_qkv[:, 1]), cosine, sine).astype(bf16)
    query_rows = query_heads.reshape(rows, width_here) * jnp.asarray(scale, bf16)
    kv = jnp.concatenate(
        [key_heads.reshape(rows, width_here), mixed_qkv[:, 2].astype(bf16)], axis=1
    )
    kv_all, attended, log_total = forward_attention(query_rows, kv, devices, 1)
    attended_low = attended.astype(bf16)
    branch = head_sum(nt(attended_low, out_turned), 2)
    middle = inputs + branch
    normed_mlp, second_pull = jax.vjp(layer_norm, middle, gain_second)
    normed_mlp = normed_mlp.astype(bf16)
    gate_up = nn(normed_mlp, full_in).reshape(rows, 2, hidden_here)

    def activate(first, second):
        return jax.nn.gelu(first, approximate=False) * second

    hidden_values, activate_pull = jax.vjp(activate, gate_up[:, 0], gate_up[:, 1])
    hidden = hidden_values.astype(bf16)
    grad_hidden = nn(cotangent, down_turned)
    grad_pair = jnp.concatenate(activate_pull(grad_hidden), axis=1).astype(bf16)
    sums = head_sum(
        jnp.concatenate([nt(hidden, down_turned), nt(grad_pair, full_in)], axis=1), 3
    )
    mixed = (middle + sums[:, :wide]).astype(bf16)
    grad_middle_norm, grad_gain_mlp = second_pull(sums[:, wide:])
    grad_middle = cotangent.astype(f32) + grad_middle_norm
    grad_attn = grad_middle.astype(bf16)
    grad_rows = nn(grad_attn, out_turned).astype(bf16)
    correction = jnp.sum(split_heads(grad_rows.astype(f32) * attended), axis=2)
    heads_here = width_here // HEAD_DIM
    stats = jnp.concatenate(
        [log_total, correction.T, jnp.zeros((8 - heads_here, rows), f32)], axis=0
    )
    grad_query, grad_key, grad_value = backward_attention(
        jnp.concatenate([query_rows, grad_rows], axis=1), stats, kv, kv_all, devices, 4
    )
    grad_query = unrotate(split_heads(grad_query), cosine, sine).reshape(rows, width_here)
    grad_key = unrotate(split_heads(grad_key), cosine, sine).reshape(rows, width_here)
    grad_triple = jnp.concatenate([grad_query, grad_key, grad_value], axis=1).astype(bf16)
    grad_normed = head_sum(nt(grad_triple, full_qkv), 5)
    _, first_pull = jax.vjp(layer_norm, inputs, gain_first)
    grad_input_norm, grad_gain_attn = first_pull(grad_normed)
    grad_tokens = grad_middle + grad_input_norm

    def tn(a, b):
        return lax.dot_general(a, b, (((0,), (0,)), ((), ())), preferred_element_type=f32)

    parts = jnp.concatenate(
        [
            tn(normed, grad_triple).astype(bf16),
            tn(normed_mlp, grad_pair).astype(bf16),
            tn(grad_attn, attended_low).astype(bf16),
            tn(cotangent, hidden).astype(bf16),
            grad_gain_attn[:, None].astype(bf16),
            grad_gain_mlp[:, None].astype(bf16),
            jnp.zeros((wide, spare), bf16),
        ],
        axis=1,
    ).reshape(devices, own, -1)
    owned = reduce_scatter(parts, devices, 6)
    cut = [owned[:, marks[i] : marks[i + 1]] for i in range(6)]
    return (
        mixed,
        grad_tokens,
        cut[0].reshape(own, 3, width_here),
        cut[2].T,
        cut[1].reshape(own, 2, hidden_here),
        cut[3].T,
        cut[4][:, 0],
        cut[5][:, 0],
    )


def solution(mesh):
    in_specs = (
        P("ctx", None),
        P("ctx", None, "head"),
        P("head", "ctx"),
        P("ctx", None, "head"),
        P("head", "ctx"),
        P("ctx"),
        P("ctx"),
        P("ctx", None),
    )
    out_specs = (
        P("ctx", None),
        P("ctx", None),
        P("ctx", None, "head"),
        P("head", "ctx"),
        P("ctx", None, "head"),
        P("head", "ctx"),
        P("ctx"),
        P("ctx"),
    )
    return jax.shard_map(
        functools.partial(shards, mesh.shape["ctx"]),
        mesh=mesh, in_specs=in_specs, out_specs=out_specs, check_vma=False,
    )
```

```python
import functools

import jax
import jax.numpy as jnp
from jax import lax
from jax.experimental import pallas as pl
from jax.experimental.pallas import tpu as pltpu
from jax.sharding import PartitionSpec as P

HEAD_DIM = 64
PAIR = 2 * HEAD_DIM
MESH = pl.DeviceIdType.MESH
VMEM_LIMIT = 56 * 1024 * 1024
RESIDENT_LIMIT = 32 * 1024 * 1024

rope_base = 160000.0
epsilon = 1e-05
f32 = jnp.float32
bf16 = jnp.bfloat16


def layer_norm(values, gain):
    centred = values - jnp.mean(values, axis=-1, keepdims=True)
    spread = jnp.mean(centred * centred, axis=-1, keepdims=True)
    return centred * lax.rsqrt(spread + epsilon) * gain


def rope_tables(first, rows):
    positions = (first + jnp.arange(rows, dtype=jnp.int32)).astype(f32)
    exponent = jnp.arange(HEAD_DIM // 2, dtype=jnp.int32).astype(f32) * (2.0 / HEAD_DIM)
    inverse = rope_base ** (-exponent)
    angles = positions[:, None] * inverse[None, :]
    angles = jnp.concatenate([angles, angles], axis=1)[:, None, :]
    return (jnp.cos(angles), jnp.sin(angles))


def turn_half(values):
    half = values.shape[-1] // 2
    return jnp.concatenate([-values[..., half:], values[..., :half]], axis=-1)


def rotate(values, cosine, sine):
    return values * cosine + turn_half(values) * sine


def unrotate(values, cosine, sine):
    return values * cosine - turn_half(values) * sine


def split_heads(flat_rows):
    return flat_rows.reshape(flat_rows.shape[0], -1, HEAD_DIM)


class Ring:
    def __init__(self, devices):
        self.chips = devices // 2
        self.half = self.chips // 2
        self.me = lax.axis_index("ctx")
        self.head = lax.axis_index("head")
        chip = lax.div(self.me, 2)
        self.core = lax.rem(self.me, 2)
        side = lax.rem(chip, 2)
        level = lax.div(chip, 2)
        self.place = level + side * (self.chips - 1 - 2 * level)

    def chip_at(self, place):
        place = lax.rem(place + 2 * self.chips, self.chips)
        far = lax.div(place, self.chips // 2)
        return (1 - far) * 2 * place + far * (2 * (self.chips - 1 - place) + 1)

    def index(self, offset, core):
        return self.chip_at(self.place + offset) * 2 + core

    def neighbours(self):
        return (self.index(1, self.core), self.index(-1, self.core), self.me + 1 - 2 * self.core)

    def barrier(self, across=False):
        sem = pltpu.get_barrier_semaphore()
        for other in self.neighbours():
            pl.semaphore_signal(sem, inc=1, device_id=(other, self.head), device_id_type=MESH)
        if across:
            pl.semaphore_signal(
                sem, inc=1, device_id=(self.me, 1 - self.head), device_id_type=MESH
            )
        pl.semaphore_wait(sem, 4 if across else 3)


def turns(ring, which):
    return (ring.half, ring.half - 1) if which % 2 == 0 else (ring.half - 1, ring.half)


class Gather:
    def __init__(self, ring, own, full, send, recv, local):
        self.ring, self.own, self.full = ring, own, full
        self.send, self.recv, self.local = send, recv, local
        self.right, self.left, self.sibling = ring.neighbours()

    def copy(self, a, kind, number, slot, target, first=False):
        return pltpu.make_async_remote_copy(
            src_ref=self.own[a] if first else self.full[a].at[slot],
            dst_ref=self.full[a].at[slot],
            send_sem=self.send.at[a, kind, number],
            recv_sem=self.recv.at[a, kind, number],
            device_id=(target, self.ring.head),
            device_id_type=MESH,
        )

    def arrive(self, a, kind, number, slot):
        self.copy(a, kind, number, slot, self.sibling).wait_recv()

    def begin(self):
        ring = self.ring
        locals_ = []
        for a in range(len(self.own)):
            rights, lefts = turns(ring, a)
            if rights:
                self.copy(a, 0, 0, ring.me, self.right, True).start()
            if lefts:
                self.copy(a, 1, 0, ring.me, self.left, True).start()
            self.copy(a, 2, 0, ring.me, self.sibling, True).start()
        for a in range(len(self.own)):
            copy = pltpu.make_async_copy(
                self.own[a], self.full[a].at[ring.me], self.local.at[a]
            )
            copy.start()
            locals_.append(copy)
        for copy in locals_:
            copy.wait()

    def step(self, s):
        ring = self.ring

        def onward(a, kind, hops, number, offset, target):
            @pl.when(s <= hops)
            def _():
                slot = ring.index(offset, ring.core)
                self.arrive(a, kind, s - 1, slot)

                @pl.when(s < hops)
                def _():
                    self.copy(a, kind, s, slot, target).start()

                self.copy(a, 2, number, slot, self.sibling).start()

        for a in range(len(self.own)):
            rights, lefts = turns(ring, a)
            onward(a, 0, rights, s, -s, self.right)
            onward(a, 1, lefts, rights + s, s, self.left)

    def sibling_step(self, s):
        ring = self.ring

        def come(a, hops, number, offset):
            @pl.when(s <= hops)
            def _():
                self.arrive(a, 2, number, ring.index(offset, 1 - ring.core))

        for a in range(len(self.own)):
            rights, lefts = turns(ring, a)
            come(a, rights, s, -s)
            come(a, lefts, rights + s, s)

    def sibling_first(self):
        for a in range(len(self.own)):
            self.arrive(a, 2, 0, self.sibling)

    def finish(self):
        ring = self.ring

        def sent(a, kind):
            def one(number, carry):
                self.copy(a, kind, number, ring.me, self.sibling).wait_send()
                return carry

            return one

        for a in range(len(self.own)):
            rights, lefts = turns(ring, a)
            lax.fori_loop(0, rights, sent(a, 0), 0)
            lax.fori_loop(0, lefts, sent(a, 1), 0)
            lax.fori_loop(0, ring.chips, sent(a, 2), 0)


class Scatter:
    def __init__(self, ring, parts, outs, stages, froms, send, recv):
        self.ring, self.parts, self.outs = ring, parts, outs
        self.stages, self.froms = stages, froms
        self.send, self.recv = send, recv
        self.right, self.left, self.sibling = ring.neighbours()

    def make(self, a, source, target, kind, number, device):
        return pltpu.make_async_remote_copy(
            src_ref=source, dst_ref=target,
            send_sem=self.send.at[a, kind, number], recv_sem=self.recv.at[a, kind, number],
            device_id=(device, self.ring.head), device_id_type=MESH,
        )

    def chip(self, a, kind, s):
        rights, lefts = turns(self.ring, a)
        return self.ring.chip_at(self.ring.place + ((rights - s) if kind == 0 else (s - lefts)))

    def over(self, a, chip):
        ring = self.ring
        return self.make(
            a, self.parts[a].at[chip * 2 + 1 - ring.core], self.stages[a].at[chip], 2, chip,
            self.sibling,
        )

    def here(self, a, chip):
        self.over(a, chip).wait_recv()
        return self.stages[a][chip].astype(f32) + self.parts[a][
            chip * 2 + self.ring.core
        ].astype(f32)

    def begin(self):
        def launch(s, carry):
            for a in range(len(self.parts)):
                for kind in range(2):
                    @pl.when(s < turns(self.ring, a)[kind])
                    def _():
                        self.over(a, self.chip(a, kind, s)).start()

            return carry

        lax.fori_loop(0, self.ring.half, launch, 0)
        for a in range(len(self.parts)):
            self.over(a, self.ring.chip_at(self.ring.place)).start()

    def first(self):
        for a in range(len(self.parts)):
            for kind in range(2):
                if turns(self.ring, a)[kind]:
                    chip = self.chip(a, kind, 0)
                    self.stages[a][chip] = self.here(a, chip).astype(bf16)
                    self.make(
                        a, self.stages[a].at[chip], self.froms[a].at[kind, 0], kind, 0,
                        (self.right, self.left)[kind],
                    ).start()

    def landed(self, a, kind, number):
        ref = self.froms[a].at[kind, number]
        self.make(a, ref, ref, kind, number, self.right).wait_recv()
        return self.froms[a][kind, number].astype(f32)

    def step(self, s):
        def onward(a, kind):
            @pl.when(s < turns(self.ring, a)[kind])
            def _():
                own = self.here(a, self.chip(a, kind, s))
                total = own + self.landed(a, kind, s - 1)
                self.froms[a][kind, s - 1] = total.astype(bf16)
                self.make(
                    a, self.froms[a].at[kind, s - 1], self.froms[a].at[kind, s], kind, s,
                    (self.right, self.left)[kind],
                ).start()

        for a in range(len(self.parts)):
            for kind in range(2):
                onward(a, kind)

    def last(self):
        ring = self.ring
        for a in range(len(self.parts)):
            total = self.here(a, ring.chip_at(ring.place))
            for kind in range(2):
                hops = turns(ring, a)[kind]
                if hops:
                    total = total + self.landed(a, kind, hops - 1)
            self.outs[a][...] = total

    def finish(self):
        def sent(a, kind):
            def one(number, carry):
                ref = self.froms[a].at[0, 0]
                self.make(a, ref, ref, kind, number, self.right).wait_send()
                return carry

            return one

        for a in range(len(self.parts)):
            for kind in range(2):
                lax.fori_loop(0, turns(self.ring, a)[kind], sent(a, kind), 0)
            lax.fori_loop(0, self.ring.chips, sent(a, 2), 0)


def scatter_scratch(parts, devices):
    chips = devices // 2
    count = len(parts)
    return (
        [pltpu.VMEM((chips,) + part.shape[1:], bf16) for part in parts]
        + [pltpu.VMEM((2, chips // 2) + part.shape[1:], bf16) for part in parts]
        + [pltpu.SemaphoreType.DMA((count, 3, chips)), pltpu.SemaphoreType.DMA((count, 3, chips))]
    )


def gather_sems(arrays, devices):
    chips = devices // 2
    return [
        pltpu.SemaphoreType.DMA((arrays, 3, chips)),
        pltpu.SemaphoreType.DMA((arrays, 3, chips)),
        pltpu.SemaphoreType.DMA((arrays,)),
    ]


def params(number):
    return pltpu.CompilerParams(
        collective_id=number, has_side_effects=True, vmem_limit_bytes=VMEM_LIMIT
    )


whole_vmem = pl.BlockSpec(memory_space=pltpu.VMEM)
whole_any = pl.BlockSpec(memory_space=pl.ANY)


def gather_kernel(devices, count, *refs):
    ring = Ring(devices)
    ring.barrier()
    gather = Gather(ring, refs[:count], refs[count : 2 * count], *refs[2 * count :])
    gather.begin()
    gather.sibling_first()

    def step(s, carry):
        gather.step(s)
        return carry

    lax.fori_loop(1, ring.half + 1, step, 0)

    def late(s, carry):
        gather.sibling_step(s)
        return carry

    lax.fori_loop(1, ring.half + 1, late, 0)
    gather.finish()


def all_gather(own, devices, number):
    return pl.pallas_call(
        functools.partial(gather_kernel, devices, len(own)),
        out_shape=tuple(jax.ShapeDtypeStruct((devices,) + x.shape, x.dtype) for x in own),
        in_specs=[whole_any] * len(own),
        out_specs=tuple([whole_any] * len(own)),
        scratch_shapes=gather_sems(len(own), devices),
        compiler_params=params(number),
    )(*own)


def nt(a, b):
    return lax.dot_general(a, b, (((1,), (1,)), ((), ())), preferred_element_type=f32)


def nn(a, b):
    return jnp.dot(a, b, preferred_element_type=f32)


def lane_mask(rows, side):
    lanes = lax.broadcasted_iota(jnp.int32, (rows, PAIR), 1)
    return (lanes >= HEAD_DIM) if side else (lanes < HEAD_DIM)


def masked_heads(source, offset, heads, target):
    for h in range(heads):
        start = offset + (h // 2) * PAIR
        block = source[:, start : start + PAIR].astype(f32)
        keep = lane_mask(block.shape[0], h % 2)
        target[h] = jnp.where(keep, block, 0.0).astype(bf16)


def fetch(sources, targets, sems):
    copies = [
        pltpu.make_async_copy(source, target, sems.at[i])
        for i, (source, target) in enumerate(zip(sources, targets))
    ]
    for copy in copies:
        copy.start()
    for copy in copies:
        copy.wait()


def visit(ring, gather, process, scatter=None):
    gather.begin()
    if scatter:
        scatter.begin()
        scatter.first()

    def opening(other, carry):
        @pl.when(other == 1)
        def _():
            gather.sibling_first()

        process(ring.index(0, ring.core + other * (1 - 2 * ring.core)))
        return carry

    lax.fori_loop(0, 2, opening, 0)

    def step(s, carry):
        gather.step(s)

        def half(other, carry):
            @pl.when(other == 1)
            def _():
                gather.sibling_step(s)
                if scatter:
                    @pl.when(s < ring.half)
                    def _():
                        scatter.step(s)

            core = ring.core + other * (1 - 2 * ring.core)
            ways = jnp.where(s < ring.half, 2, 1)

            def way(w, carry):
                process(ring.index((2 * w - 1) * s, core))
                return carry

            return lax.fori_loop(0, ways, way, carry)

        return lax.fori_loop(0, 2, half, carry)

    lax.fori_loop(1, ring.half + 1, step, 0)
    gather.finish()
    if scatter:
        scatter.last()
        scatter.finish()


def forward_kernel(
    devices, heads, q, k, v, full_k, full_v, att, lse, qm, top, total, acc, send, recv, local, *stage
):
    ring = Ring(devices)
    ring.barrier()
    gather = Gather(ring, [k, v], [full_k, full_v], send, recv, local)
    masked_heads(q, 0, heads, qm)
    top[...] = jnp.full_like(top, -1e30)
    total[...] = jnp.zeros_like(total)
    acc[...] = jnp.zeros_like(acc)

    def process(slot):
        keyed, valued = full_k.at[slot], full_v.at[slot]
        if stage:
            fetch((keyed, valued), stage[:2], stage[2])
            keyed, valued = stage[:2]
        for p in range(heads // 2):
            keys = keyed[:, p * PAIR : (p + 1) * PAIR]
            values = valued[:, p * PAIR : (p + 1) * PAIR].T
            for side in range(2):
                h = 2 * p + side
                scores = nt(keys, qm[h])
                before = top[h : h + 1]
                peak = jnp.maximum(before, jnp.max(scores, axis=0, keepdims=True))
                shrink = jnp.exp(before - peak)
                weights = jnp.exp(scores - peak)
                top[h : h + 1] = peak
                total[h : h + 1] = total[h : h + 1] * shrink + jnp.sum(
                    weights, axis=0, keepdims=True
                )
                part = nn(values[side * HEAD_DIM : (side + 1) * HEAD_DIM], weights.astype(bf16))
                rows = slice(h * HEAD_DIM, (h + 1) * HEAD_DIM)
                acc[rows] = acc[rows] * shrink + part

    visit(ring, gather, process)
    for h in range(heads):
        rows = slice(h * HEAD_DIM, (h + 1) * HEAD_DIM)
        acc[rows] = acc[rows] / total[h : h + 1]
    att[...] = acc[...].T
    lse[...] = top[...] + jnp.log(jnp.maximum(total[...], 1e-37))


def resident(devices, rows, width):
    return devices * rows * width * 2 * 2 <= RESIDENT_LIMIT


def forward_attention(q, k, v, devices, number):
    rows, width = q.shape
    heads = width // HEAD_DIM
    near = resident(devices, rows, 2 * width)
    space = whole_vmem if near else whole_any
    full = jax.ShapeDtypeStruct((devices,) + k.shape, bf16)
    return pl.pallas_call(
        functools.partial(forward_kernel, devices, heads),
        out_shape=(
            full,
            full,
            jax.ShapeDtypeStruct((rows, width), f32),
            jax.ShapeDtypeStruct((8, rows), f32),
        ),
        in_specs=[whole_vmem, space, space],
        out_specs=(space, space, whole_vmem, whole_vmem),
        scratch_shapes=[
            pltpu.VMEM((heads, rows, PAIR), bf16),
            pltpu.VMEM((8, rows), f32),
            pltpu.VMEM((8, rows), f32),
            pltpu.VMEM((width, rows), f32),
        ]
        + gather_sems(2, devices)
        + (
            []
            if near
            else [
                pltpu.VMEM(k.shape, bf16),
                pltpu.VMEM(v.shape, bf16),
                pltpu.SemaphoreType.DMA((2,)),
            ]
        ),
        compiler_params=params(number),
    )(q, k, v)


def unturn(block, cosine, sine):
    half = HEAD_DIM // 2
    low, high = block[:half], block[half:]
    return jnp.concatenate(
        [low * cosine + high * sine, high * cosine - low * sine], axis=0
    )


def backward_kernel(devices, heads, near, count, *refs):
    q, g, stats, k, v, k_all, v_all, cosine, sine, lonely = refs[:10]
    parts = refs[10 : 10 + count]
    rest = refs[10 + count :]
    triple, joined = rest[:2]
    outs = rest[2 : 2 + count]
    rest = rest[2 + count :]
    q_all, g_all, stats_all = rest[:3]
    qm, gm, km, vm, dqt, dka, dva, send, recv, local = rest[3:13]
    stages = rest[13 : 13 + count]
    froms = rest[13 + count : 13 + 2 * count]
    scatter_send, scatter_recv, met, met_send, met_recv = rest[13 + 2 * count : 18 + 2 * count]
    stage = rest[18 + 2 * count :]
    width = heads * HEAD_DIM
    ring = Ring(devices)
    ring.barrier(True)
    meet = pltpu.make_async_remote_copy(
        src_ref=lonely, dst_ref=met, send_sem=met_send, recv_sem=met_recv,
        device_id=(ring.me, 1 - ring.head), device_id_type=MESH,
    )
    meet.start()
    gather = Gather(ring, [q, g, stats], [q_all, g_all, stats_all], send, recv, local)
    scatter = Scatter(ring, parts, outs, stages, froms, scatter_send, scatter_recv)
    own_q, own_g, mine = q, g, stats
    if stage:
        fetch((q, g, stats), (stage[0], stage[1], stage[6]), stage[5])
        own_q, own_g, mine = stage[0], stage[1], stage[6]
    masked_heads(own_q, 0, heads, qm)
    masked_heads(own_g, 0, heads, gm)
    masked_heads(k, 0, heads, km)
    masked_heads(v, 0, heads, vm)
    dqt[...] = jnp.zeros_like(dqt)
    dka[...] = jnp.zeros_like(dka)
    dva[...] = jnp.zeros_like(dva)

    def process(slot):
        asked, graded, rows_of = q_all.at[slot], g_all.at[slot], stats_all.at[slot]
        keyed, valued = k_all.at[slot], v_all.at[slot]
        if stage:
            fetch((asked, graded, rows_of, keyed, valued), stage[:5], stage[5])
            asked, graded, rows_of, keyed, valued = stage[:5]
        for p in range(heads // 2):
            span = slice(p * PAIR, (p + 1) * PAIR)
            keys = keyed[:, span]
            values = valued[:, span]
            turned = keys.T
            queries = asked[:, span]
            grads = graded[:, span]
            for side in range(2):
                h = 2 * p + side
                probs = jnp.exp(nt(keys, qm[h]) - mine[h : h + 1])
                slope = nt(values, gm[h])
                small = (probs * (slope - mine[8 + h : 9 + h])).astype(bf16)
                rows = slice(h * HEAD_DIM, (h + 1) * HEAD_DIM)
                dqt[rows] += nn(turned[side * HEAD_DIM : (side + 1) * HEAD_DIM], small)
                probs = jnp.exp(nt(km[h], queries) - rows_of[h : h + 1])
                slope = nt(vm[h], grads)
                small = (probs * (slope - rows_of[8 + h : 9 + h])).astype(bf16)
                dva[h] += nn(probs.astype(bf16), grads)
                dka[h] += nn(small, queries)

    visit(ring, gather, process, scatter)
    meet.wait()
    joined[...] = lonely[...].astype(f32) + met[...].astype(f32)
    keep = lane_mask(triple.shape[0], 0)
    scale = HEAD_DIM ** (-0.5)
    for p in range(heads // 2):
        for which in range(2):
            if which == 0:
                block = dqt[p * PAIR : (p + 1) * PAIR] * scale
            else:
                block = jnp.where(keep, dka[2 * p], dka[2 * p + 1]).T
            block = jnp.concatenate(
                [
                    unturn(block[:HEAD_DIM], cosine[...], sine[...]),
                    unturn(block[HEAD_DIM:], cosine[...], sine[...]),
                ],
                axis=0,
            )
            start = which * width + p * PAIR
            triple[:, start : start + PAIR] = block.T.astype(bf16)
        start = 2 * width + p * PAIR
        triple[:, start : start + PAIR] = jnp.where(keep, dva[2 * p], dva[2 * p + 1]).astype(bf16)


def backward_attention(q, g, stats, k, v, k_all, v_all, cosine, sine, lonely, parts, devices, number):
    rows, width = q.shape
    heads = width // HEAD_DIM
    near = resident(devices, rows, 2 * width)
    gathered = [(q.shape, bf16), (g.shape, bf16), (stats.shape, f32)]
    gathered = [((devices,) + shape, kind) for shape, kind in gathered]
    out_shape = [
        jax.ShapeDtypeStruct((rows, 3 * width), bf16),
        jax.ShapeDtypeStruct(lonely.shape, f32),
    ] + [jax.ShapeDtypeStruct(part.shape[1:], f32) for part in parts]
    out_specs = [whole_vmem] * len(out_shape)
    kept = len(out_shape)
    buffers = []
    if near:
        buffers = [pltpu.VMEM(shape, kind) for shape, kind in gathered]
    else:
        out_shape += [jax.ShapeDtypeStruct(shape, kind) for shape, kind in gathered]
        out_specs += [whole_any] * 3
    space = whole_vmem if near else whole_any
    return pl.pallas_call(
        functools.partial(backward_kernel, devices, heads, near, len(parts)),
        out_shape=tuple(out_shape),
        in_specs=[space] * 3 + [whole_vmem] * 2 + [space] * 2 + [whole_vmem] * (3 + len(parts)),
        out_specs=tuple(out_specs),
        scratch_shapes=buffers
        + [pltpu.VMEM((heads, rows, PAIR), bf16)] * 4
        + [
            pltpu.VMEM((width, rows), f32),
            pltpu.VMEM((heads, rows, PAIR), f32),
            pltpu.VMEM((heads, rows, PAIR), f32),
        ]
        + gather_sems(3, devices)
        + scatter_scratch(parts, devices)
        + [pltpu.VMEM(lonely.shape, bf16), pltpu.SemaphoreType.DMA, pltpu.SemaphoreType.DMA]
        + (
            []
            if near
            else [
                pltpu.VMEM(q.shape, bf16),
                pltpu.VMEM(g.shape, bf16),
                pltpu.VMEM(stats.shape, f32),
                pltpu.VMEM(k.shape, bf16),
                pltpu.VMEM(v.shape, bf16),
                pltpu.SemaphoreType.DMA((5,)),
                pltpu.VMEM(stats.shape, f32),
            ]
        ),
        compiler_params=params(number),
    )(q, g, stats, k, v, k_all, v_all, cosine, sine, lonely, *parts)[:kept]


def exchange_kernel(own, out, arrived, send, recv):
    other = 1 - lax.axis_index("head")
    here = lax.axis_index("ctx")
    sem = pltpu.get_barrier_semaphore()
    pl.semaphore_signal(sem, inc=1, device_id=(here, other), device_id_type=MESH)
    pl.semaphore_wait(sem, 1)
    copy = pltpu.make_async_remote_copy(
        src_ref=own, dst_ref=arrived, send_sem=send, recv_sem=recv,
        device_id=(here, other), device_id_type=MESH,
    )
    copy.start()
    copy.wait()
    out[...] = own[...].astype(f32) + arrived[...].astype(f32)


def head_sum(part, number):
    part = part.astype(bf16)
    return pl.pallas_call(
        exchange_kernel,
        out_shape=jax.ShapeDtypeStruct(part.shape, f32),
        in_specs=[whole_vmem],
        out_specs=whole_vmem,
        scratch_shapes=[
            pltpu.VMEM(part.shape, bf16), pltpu.SemaphoreType.DMA, pltpu.SemaphoreType.DMA,
        ],
        compiler_params=params(number),
    )(part)


def scatter_kernel(devices, count, *refs):
    ring = Ring(devices)
    ring.barrier()
    cut = [refs[i * count : (i + 1) * count] for i in range(4)]
    scatter = Scatter(ring, *cut, *refs[4 * count :])
    scatter.begin()
    scatter.first()

    def step(s, carry):
        scatter.step(s)
        return carry

    lax.fori_loop(1, ring.half, step, 0)
    scatter.last()
    scatter.finish()


def reduce_scatter(parts, devices, number):
    return pl.pallas_call(
        functools.partial(scatter_kernel, devices, len(parts)),
        out_shape=tuple(jax.ShapeDtypeStruct(part.shape[1:], f32) for part in parts),
        in_specs=[whole_vmem] * len(parts),
        out_specs=tuple([whole_vmem] * len(parts)),
        scratch_shapes=scatter_scratch(parts, devices),
        compiler_params=params(number),
    )(*parts)


def shards(devices, tokens, w_qkv, w_out, w_in, w_down, gain_attn, gain_mlp, cotangent):
    rows, wide = tokens.shape
    own = w_qkv.shape[0]
    scale = HEAD_DIM ** (-0.5)
    width_here = w_qkv.shape[2]
    hidden_here = w_in.shape[2]
    gains = jnp.concatenate(
        [gain_attn[:, None], gain_mlp[:, None], jnp.zeros((own, 126), bf16)], axis=1
    )
    full_qkv, full_in, out_turned, down_turned, full_gains = (
        x.reshape(wide, -1)
        for x in all_gather(
            (w_qkv.reshape(own, -1), w_in.reshape(own, -1), w_out.T, w_down.T, gains), devices, 0
        )
    )
    gain_first = full_gains[:, 0].astype(f32)
    gain_second = full_gains[:, 1].astype(f32)
    cosine, sine = rope_tables(lax.axis_index("ctx") * rows, rows)
    inputs = tokens.astype(f32)
    normed = layer_norm(inputs, gain_first).astype(bf16)
    mixed_qkv = nn(normed, full_qkv).reshape(rows, 3, width_here)
    query_heads = rotate(split_heads(mixed_qkv[:, 0]), cosine, sine).astype(bf16)
    key_heads = rotate(split_heads(mixed_qkv[:, 1]), cosine, sine).astype(bf16)
    query_rows = query_heads.reshape(rows, width_here) * jnp.asarray(scale, bf16)
    key_rows = key_heads.reshape(rows, width_here)
    value_rows = mixed_qkv[:, 2].astype(bf16)
    keys_all, values_all, attended, log_total = forward_attention(
        query_rows, key_rows, value_rows, devices, 1
    )
    attended_low = attended.astype(bf16)
    branch = head_sum(nt(attended_low, out_turned), 2)
    middle = inputs + branch
    normed_mlp, second_pull = jax.vjp(layer_norm, middle, gain_second)
    normed_mlp = normed_mlp.astype(bf16)
    gate_up = nn(normed_mlp, full_in).reshape(rows, 2, hidden_here)

    def activate(first, second):
        return jax.nn.gelu(first, approximate=False) * second

    hidden_values, activate_pull = jax.vjp(activate, gate_up[:, 0], gate_up[:, 1])
    hidden = hidden_values.astype(bf16)
    grad_hidden = nn(cotangent, down_turned)
    grad_pair = jnp.concatenate(activate_pull(grad_hidden), axis=1).astype(bf16)
    grad_normed_mlp = head_sum(nt(grad_pair, full_in), 3)
    grad_middle_norm, grad_gain_mlp = second_pull(grad_normed_mlp)
    grad_middle = cotangent.astype(f32) + grad_middle_norm
    grad_attn = grad_middle.astype(bf16)
    grad_rows = nn(grad_attn, out_turned).astype(bf16)
    correction = jnp.sum(split_heads(grad_rows.astype(f32) * attended), axis=2)
    heads_here = width_here // HEAD_DIM
    stats = jnp.concatenate(
        [log_total, correction.T, jnp.zeros((8 - heads_here, rows), f32)], axis=0
    )

    def tn(a, b):
        return lax.dot_general(
            a, b, (((0,), (0,)), ((), ())), preferred_element_type=f32
        ).astype(bf16)

    def blocks(part):
        return part.reshape(devices, own, -1)

    def with_gain(part, gain):
        return jnp.concatenate(
            [part, gain[:, None].astype(bf16), jnp.zeros((wide, 127), bf16)], axis=1
        )

    early = (
        blocks(tn(normed_mlp, grad_pair)),
        blocks(tn(cotangent, hidden)),
        blocks(with_gain(tn(grad_attn, attended_low), grad_gain_mlp)),
    )
    half = HEAD_DIM // 2
    grad_triple, branch_mlp, owned_in, owned_down, owned_out = backward_attention(
        query_rows, grad_rows, stats, key_rows, value_rows, keys_all, values_all,
        cosine[:, 0, :half].T, sine[:, 0, :half].T,
        nt(hidden, down_turned).astype(bf16), early, devices, 4,
    )
    mixed = (middle + branch_mlp).astype(bf16)
    grad_normed = head_sum(nt(grad_triple, full_qkv), 5)
    _, first_pull = jax.vjp(layer_norm, inputs, gain_first)
    grad_input_norm, grad_gain_attn = first_pull(grad_normed)
    grad_tokens = grad_middle + grad_input_norm

    cut = (3 * width_here // 2) // 128 * 128 + 128 * (3 * width_here % 256 > 0)
    owned_first, owned_second = reduce_scatter(
        (
            blocks(tn(normed, grad_triple[:, :cut])),
            blocks(with_gain(tn(normed, grad_triple[:, cut:]), grad_gain_attn)),
        ),
        devices,
        6,
    )
    rest = 3 * width_here - cut
    owned_qkv = jnp.concatenate([owned_first, owned_second[:, :rest]], axis=1)
    return (
        mixed,
        grad_tokens,
        owned_qkv.reshape(own, 3, width_here),
        owned_out[:, :width_here].T,
        owned_in.reshape(own, 2, hidden_here),
        owned_down.T,
        owned_second[:, rest],
        owned_out[:, width_here],
    )


def solution(mesh):
    in_specs = (
        P("ctx", None),
        P("ctx", None, "head"),
        P("head", "ctx"),
        P("ctx", None, "head"),
        P("head", "ctx"),
        P("ctx"),
        P("ctx"),
        P("ctx", None),
    )
    out_specs = (
        P("ctx", None),
        P("ctx", None),
        P("ctx", None, "head"),
        P("head", "ctx"),
        P("ctx", None, "head"),
        P("head", "ctx"),
        P("ctx"),
        P("ctx"),
    )
    return jax.shard_map(
        functools.partial(shards, mesh.shape["ctx"]),
        mesh=mesh, in_specs=in_specs, out_specs=out_specs, check_vma=False,
    )
```
